512 devices in a mesh: ctx: 32 (over z_lo, y, core), head: 16 (over x, z_hi).
Axes of the slice: x: 4, y: 4, z: 16 (z_hi: 4, z_lo: 4; z = z_hi * 4 + z_lo), core: 2. Of those that a mesh axis runs over, the one named last changes fastest.
Arguments:
- q_nope: bfloat16 [4096, 16384], P('ctx', 'head'), may hold values from -6 to 6
- q_rope: bfloat16 [4096, 8192], P('ctx', 'head'), may hold values from -250 to 250
- latent: bfloat16 [4096, 512], P('ctx'), may hold values from -6 to 6
- k_rope: bfloat16 [4096, 64], P('ctx'), may hold values from -5 to 5
- d_out: bfloat16 [4096, 16384], P('ctx', 'head'), may hold values from -6 to 6
- advantage: float32 [4096], P('ctx'), may hold values from -4 to 4
- segment: int32 [4096], replicated, may hold values from 0 to 31, never falling along the last dimension, each value on 1 to 512 neighbouring positions
- w_uk: bfloat16 [512, 16384], P('ctx', 'head'), may hold values from -0.5 to 0.5
- w_uv: bfloat16 [512, 16384], P('ctx', 'head'), may hold values from -0.5 to 0.5
Outputs:
- d_q_nope: bfloat16 [4096, 16384], P('ctx', 'head')
- d_q_rope: bfloat16 [4096, 8192], P('ctx', 'head')
- d_latent: float32 [4096, 512], P(('ctx', 'head'))
- d_k_rope: float32 [4096, 64], P(('ctx', 'head'))
- d_w_uk: float32 [512, 16384], P('ctx', 'head')
- d_w_uv: float32 [512, 16384], P('ctx', 'head')
The draws below stay inside these ranges and needn't reach their ends.
Inputs may be any that keep to these rules, and one draw needn't show every extreme that they name: Segment numbers never fall; each segment holds 1 to 512 tokens and one holds exactly 512.
All inputs are finite; a program needn't handle non-finite values.
Results may differ from the reference program's by a relative error of at most 0.03.
Values may be sent and summed in bfloat16 or wider, within the bound.
No kernel may reach another device: no remote copies, remote signals or barrier semaphores. Data moves between devices by JAX's collectives and lax.ppermute only.
A program may use at most 64 MiB of HBM per device.

```python
import math
import jax
import jax.numpy as jnp
import numpy as np
from jax import lax

LAT = 512
ROPE = 64
NOPE = 128
VDIM = 128
TOK_DEV = 128
HEADS = 128
TOKENS = 4096
SEG_MOST = 512
SEG_COUNT = 32
N_CTX = 32


def shared_rope(key):
    return jax.random.truncated_normal(jax.random.fold_in(key, 7), -4.0, 4.0, (TOKENS, ROPE), jnp.float32)


def draw_k_rope(key, part):
    shared = shared_rope(key)
    return shared.astype(jnp.bfloat16)


def draw_q_rope(key, part):
    key = jax.random.fold_in(key, 2)
    values = jax.random.truncated_normal(key, -4.0, 4.0, (TOKENS, HEADS * ROPE), jnp.float32)
    return values.astype(jnp.bfloat16)


def shard_levels(rng, extent, cuts, smallest, largest):
    loudness = 1.0
    for axis_at, shards_of in cuts:
        draws = jax.random.uniform(jax.random.fold_in(jax.random.fold_in(rng, 6), axis_at), (shards_of,), jnp.float32, smallest / len(cuts), largest / len(cuts))
        loudness = loudness * jnp.repeat(jnp.exp(draws), extent[axis_at] // shards_of).reshape((-1,) + (1,) * (len(extent) - 1 - axis_at))
    return loudness


def length_profile(amount, total, limit, slope):
    weights = [(1 << 20) // math.isqrt(rank ** slope) + 1 for rank in range(2, amount + 1)]
    surplus, counts = total - limit - (amount - 1), [1] * (amount - 1)
    while surplus > 0:
        candidates = [i for i in range(amount - 1) if counts[i] < limit]
        mass, left = sum([weights[i] for i in candidates]), surplus
        for i in candidates:
            addition = min(limit - counts[i], max(1, left * weights[i] // mass), surplus)
            counts[i] = counts[i] + addition
            surplus = surplus - addition
    return np.array([limit] + counts)


def uneven_parts(own_key, amount, total, bound, skew):
    if amount == 2:
        one = jax.random.randint(own_key, (), max(1, total - bound), min(bound, total - 1) + 1)
        return jnp.stack([one, total - one])
    tallies = jnp.asarray(length_profile(amount, total, bound, skew), jnp.int32)
    pairs = (amount - 1) // 2
    source_of, sink = tallies[1:1 + 2 * pairs:2], tallies[2:2 + 2 * pairs:2]
    margin = jnp.minimum(source_of - 1, bound - sink)
    shifted = jax.random.randint(jax.random.fold_in(own_key, 1), (pairs,), 0, 1 << 20) % (margin + 1)
    tallies = tallies.at[1:1 + 2 * pairs:2].set(source_of - shifted).at[2:2 + 2 * pairs:2].set(sink + shifted)
    return tallies[jax.random.permutation(jax.random.fold_in(own_key, 2), amount)]


def normal_values(rng, extent, width, reach, pieces=(), kind=jnp.bfloat16):
    drawn = width * jax.random.normal(rng, extent, jnp.float32)
    if pieces:
        drawn = drawn * shard_levels(rng, extent, pieces, -0.22, 0.18)
    return jnp.clip(drawn, -reach, reach).astype(kind)


def setup_inputs(seed: int = 0) -> dict:
    key_of = jax.random.split(jax.random.key(seed), 10)
    q_nope = normal_values(key_of[0], (TOKENS, HEADS * NOPE), 1.0, 6.0, ((0, 32), (1, 16)))
    q_rope = draw_q_rope(jax.random.fold_in(key_of[9], 71), 0)
    latent = normal_values(key_of[2], (TOKENS, LAT), 1.0, 6.0, ((0, 32),))
    k_rope = draw_k_rope(jax.random.fold_in(key_of[9], 71), 0)
    d_out = normal_values(key_of[4], (TOKENS, HEADS * VDIM), 1.0, 6.0, ((0, 32), (1, 16)))
    advantage = normal_values(key_of[5], (TOKENS,), 1.0, 4.0, ((0, 32),), jnp.float32)
    segment = jnp.searchsorted(jnp.cumsum(uneven_parts(key_of[6], SEG_COUNT, TOKENS, SEG_MOST, 2)), jnp.arange(TOKENS), side="right").astype(jnp.int32)
    w_uk = normal_values(key_of[7], (LAT, HEADS * NOPE), NOPE ** -0.5, 0.5, ((0, 32), (1, 16)))
    w_uv = normal_values(key_of[8], (LAT, HEADS * VDIM), VDIM ** -0.5, 0.5, ((0, 32), (1, 16)))
    return {"q_nope": q_nope, "q_rope": q_rope, "latent": latent, "k_rope": k_rope, "d_out": d_out, "advantage": advantage, "segment": segment, "w_uk": w_uk, "w_uv": w_uv}


def block_product(left, right):
    left_blocks = left.reshape(N_CTX, TOK_DEV, left.shape[1]).astype(jnp.float32)
    right_blocks = right.reshape(N_CTX, TOK_DEV, right.shape[1]).astype(jnp.float32)
    partial_sums = jnp.einsum('kta,ktn->kan', left_blocks, right_blocks)
    rounded = lax.optimization_barrier(partial_sums.astype(jnp.bfloat16))
    return lax.optimization_barrier(jnp.sum(rounded.astype(jnp.float32), axis=0))

def reference(q_nope, q_rope, latent, k_rope, d_out, advantage, segment, w_uk, w_uv):
    tokens = latent.shape[0]
    score_scale = 1.0 / math.sqrt(NOPE + ROPE)
    queries = q_nope.reshape(tokens, HEADS, NOPE).transpose(1, 0, 2)
    rotated = q_rope.reshape(tokens, HEADS, ROPE).transpose(1, 0, 2)
    cotangent = d_out.reshape(tokens, HEADS, VDIM).transpose(1, 0, 2)
    up_keys = w_uk.reshape(LAT, HEADS, NOPE).transpose(1, 0, 2)
    up_values = w_uv.reshape(LAT, HEADS, VDIM).transpose(1, 0, 2)
    places = jnp.arange(tokens, dtype=jnp.int32)
    allowed = (segment[:, None] == segment[None, :]) & (places[None, :] <= places[:, None])

    def one_head(running, sliced):
        query_h, rotated_h, cotangent_h, up_key_h, up_value_h = sliced
        weighted = (advantage[:, None] * cotangent_h.astype(jnp.float32)).astype(jnp.bfloat16)
        absorbed = jnp.dot(query_h, up_key_h.T, preferred_element_type=jnp.float32).astype(jnp.bfloat16)
        back_lat = jnp.dot(weighted, up_value_h.T, preferred_element_type=jnp.float32).astype(jnp.bfloat16)
        scores = jnp.dot(absorbed, latent.T, preferred_element_type=jnp.float32)
        scores = (scores + jnp.dot(rotated_h, k_rope.T, preferred_element_type=jnp.float32)) * score_scale
        scores = jnp.where(allowed, scores, -jnp.inf)
        row_max = lax.optimization_barrier(jnp.max(scores, axis=-1, keepdims=True))
        exponent = jnp.exp(scores - row_max)
        probs = exponent / lax.optimization_barrier(jnp.sum(exponent, axis=-1, keepdims=True))
        probs_low = probs.astype(jnp.bfloat16)
        grad_prob = jnp.dot(back_lat, latent.T, preferred_element_type=jnp.float32)
        row_delta = lax.optimization_barrier(jnp.sum(probs * grad_prob, axis=-1, keepdims=True))
        grad_score = (probs * (grad_prob - row_delta) * score_scale).astype(jnp.bfloat16)
        out_lat = jnp.dot(probs_low, latent, preferred_element_type=jnp.float32).astype(jnp.bfloat16)
        grad_abs = jnp.dot(grad_score, latent, preferred_element_type=jnp.float32).astype(jnp.bfloat16)
        grad_rot = jnp.dot(grad_score, k_rope, preferred_element_type=jnp.float32).astype(jnp.bfloat16)
        grad_query = jnp.dot(grad_abs, up_key_h, preferred_element_type=jnp.float32).astype(jnp.bfloat16)
        lat_sum = running[0] + jnp.dot(grad_score.T, absorbed, preferred_element_type=jnp.float32)
        lat_sum = lat_sum + jnp.dot(probs_low.T, back_lat, preferred_element_type=jnp.float32)
        rope_sum = running[1] + jnp.dot(grad_score.T, rotated_h, preferred_element_type=jnp.float32)
        grad_keys = block_product(grad_abs, query_h)
        grad_values = block_product(out_lat, weighted)
        return ((lat_sum, rope_sum), (grad_query, grad_rot, grad_keys, grad_values))
    start_sums = (jnp.zeros((tokens, LAT), jnp.float32), jnp.zeros((tokens, ROPE), jnp.float32))
    sums, stacked = lax.scan(one_head, start_sums, (queries, rotated, cotangent, up_keys, up_values))
    grad_query, grad_rot, grad_keys, grad_values = stacked
    d_q_nope = grad_query.transpose(1, 0, 2).reshape(tokens, HEADS * NOPE)
    d_q_rope = grad_rot.transpose(1, 0, 2).reshape(tokens, HEADS * ROPE)
    d_w_uk = grad_keys.transpose(1, 0, 2).reshape(LAT, HEADS * NOPE)
    d_w_uv = grad_values.transpose(1, 0, 2).reshape(LAT, HEADS * VDIM)
    return (d_q_nope, d_q_rope, sums[0], sums[1], d_w_uk, d_w_uv)
```

```python
import functools
import math

import jax
import jax.numpy as jnp
from jax import lax
from jax.experimental import pallas as pl
from jax.experimental.pallas import tpu as pltpu
from jax.sharding import PartitionSpec as P

LAT = 512
ROPE = 64
NOPE = 128
VDIM = 128
FAR = -1e30


def dot_nt(left, right):
    return lax.dot_general(
        left, right, (((1,), (1,)), ((), ())), preferred_element_type=jnp.float32
    )


def dot_nn(left, right):
    return lax.dot_general(
        left, right, (((1,), (0,)), ((), ())), preferred_element_type=jnp.float32
    )


def dot_tn(left, right):
    return lax.dot_general(
        left, right, (((0,), (0,)), ((), ())), preferred_element_type=jnp.float32
    )


def column_of(row, count):
    return jnp.transpose(jnp.broadcast_to(row, (count, count)))


def core_rows(value, side):
    pieces = value.reshape(value.shape[0] // 32, 2, 16, value.shape[1])
    return pieces[:, side].reshape(value.shape[0] // 2, value.shape[1])


def layer_kernel(
    place,
    advantage,
    segment,
    queries,
    rotated,
    cotangent,
    key4,
    key3,
    key2,
    key1,
    key0,
    weights_mine,
    weights_theirs,
    d_q_nope,
    d_q_rope,
    grad_earlier,
    grad_own,
    d_weights_mine,
    d_weights_theirs,
    weights,
    keys,
    keys_t,
    bias,
    absorbed,
    back_lat,
    probs_low,
    grad_score,
):
    rows = queries.shape[0]
    width = queries.shape[1]
    heads = width // NOPE
    span = keys.shape[0]
    reach = span // rows - 1
    scale = 1.0 / math.sqrt(NOPE + ROPE)
    index = place[0]
    core = lax.rem(index, 2)

    for piece in range(weights_mine.shape[0] // 16):
        source = slice(piece * 16, piece * 16 + 16)
        mine_at = pl.multiple_of(piece * 32 + core * 16, 16)
        theirs_at = pl.multiple_of(piece * 32 + 16 - core * 16, 16)
        weights[pl.ds(mine_at, 16), :] = weights_mine[source, :]
        weights[pl.ds(theirs_at, 16), :] = weights_theirs[source, :]

    for block, piece in enumerate((key4, key3, key2, key1, key0)):
        keys[block * rows : (block + 1) * rows, :] = piece[...]
        keys_t[:, block * rows : (block + 1) * rows] = jnp.transpose(piece[...])

    query_segment = segment[pl.ds(index, 1), :]
    query_at = lax.broadcasted_iota(jnp.int32, (rows, rows), 1)
    key_at = lax.broadcasted_iota(jnp.int32, (rows, rows), 0)
    for block in range(reach + 1):
        owner = index - (reach - block)
        key_row = segment[pl.ds(jnp.maximum(owner, 0), 1), :]
        key_segment = column_of(key_row, rows)
        allowed = (key_segment == query_segment) & (owner >= 0)
        if block == reach:
            allowed = allowed & (key_at <= query_at)
        bias[block * rows : (block + 1) * rows, :] = jnp.where(allowed, 0.0, FAR)

    advantage_column = column_of(advantage[...], rows)
    bias_pair = jnp.concatenate([bias[...], bias[...]], axis=1)

    for pair in range(heads // 2):
        both = slice(pair * 2 * rows, (pair + 1) * 2 * rows)
        weighted = []
        for head in (2 * pair, 2 * pair + 1):
            here = slice(head * rows, (head + 1) * rows)
            nope = slice(head * NOPE, (head + 1) * NOPE)
            values = slice(width + head * VDIM, width + (head + 1) * VDIM)
            absorbed[here, :LAT] = dot_nt(queries[:, nope], weights[:, nope]).astype(jnp.bfloat16)
            absorbed[here, LAT:] = rotated[:, head * ROPE : (head + 1) * ROPE]
            weighted.append(
                (advantage_column * cotangent[:, nope].astype(jnp.float32)).astype(jnp.bfloat16)
            )
            back_lat[here, :] = dot_nt(weighted[-1], weights[:, values]).astype(jnp.bfloat16)
        scores = dot_nt(keys[...], absorbed[both, :]) * scale + bias_pair
        exponent = jnp.exp(scores - jnp.max(scores, axis=0, keepdims=True))
        probs = exponent * (1.0 / jnp.sum(exponent, axis=0, keepdims=True))
        low = probs.astype(jnp.bfloat16)
        probs_low[:, both] = low
        grad_prob = dot_nt(keys[:, :LAT], back_lat[both, :])
        row_delta = jnp.sum(probs * grad_prob, axis=0, keepdims=True)
        score = (probs * (grad_prob - row_delta) * scale).astype(jnp.bfloat16)
        grad_score[:, both] = score
        out_lat = dot_nn(keys_t[:LAT, :], low).astype(jnp.bfloat16)
        grad_abs = dot_nn(keys_t[...], score).astype(jnp.bfloat16)
        rope_rows = grad_abs[LAT:, :].astype(jnp.float32)
        rope_rows = jnp.concatenate([rope_rows[:, :rows], rope_rows[:, rows:]], axis=0)
        d_q_rope[:, pair * 2 * ROPE : (pair + 1) * 2 * ROPE] = jnp.transpose(rope_rows).astype(
            jnp.bfloat16
        )
        for side, head in enumerate((2 * pair, 2 * pair + 1)):
            nope = slice(head * NOPE, (head + 1) * NOPE)
            values = slice(width + head * VDIM, width + (head + 1) * VDIM)
            mine = slice(side * rows, (side + 1) * rows)
            d_q_nope[:, nope] = dot_tn(grad_abs[:LAT, mine], weights[:, nope]).astype(jnp.bfloat16)
            term_keys = dot_nn(grad_abs[:LAT, mine], queries[:, nope]).astype(jnp.bfloat16)
            term_values = dot_nn(out_lat[:, mine], weighted[side]).astype(jnp.bfloat16)
            for columns, term in ((nope, term_keys), (values, term_values)):
                even, odd = core_rows(term, 0), core_rows(term, 1)
                d_weights_mine[:, columns] = jnp.where(core == 0, even, odd)
                d_weights_theirs[:, columns] = jnp.where(core == 0, odd, even)

    for block in range(reach + 1):
        here = slice(block * rows, (block + 1) * rows)
        total = dot_nn(grad_score[here, :], absorbed[...])
        total_lat = total[:, :LAT] + dot_nn(probs_low[here, :], back_lat[...])
        if block < reach:
            grad_earlier[here, :LAT] = total_lat.astype(jnp.bfloat16)
            grad_earlier[here, LAT:] = total[:, LAT:].astype(jnp.bfloat16)
        else:
            grad_own[:, :LAT] = total_lat
            grad_own[:, LAT:] = total[:, LAT:]


def layer(place, advantage, segment, queries, rotated, cotangent, key_blocks, mine, theirs):
    rows, width = queries.shape
    heads = width // NOPE
    span = len(key_blocks) * rows
    wide = LAT + ROPE
    whole = pl.BlockSpec(memory_space=pltpu.VMEM)
    return pl.pallas_call(
        layer_kernel,
        out_shape=(
            jax.ShapeDtypeStruct((rows, width), jnp.bfloat16),
            jax.ShapeDtypeStruct((rows, heads * ROPE), jnp.bfloat16),
            jax.ShapeDtypeStruct((span - rows, wide), jnp.bfloat16),
            jax.ShapeDtypeStruct((rows, wide), jnp.float32),
            jax.ShapeDtypeStruct(mine.shape, jnp.bfloat16),
            jax.ShapeDtypeStruct(theirs.shape, jnp.bfloat16),
        ),
        in_specs=[pl.BlockSpec(memory_space=pltpu.SMEM)] + [whole] * (7 + len(key_blocks)),
        out_specs=(whole,) * 6,
        scratch_shapes=[
            pltpu.VMEM((LAT, 2 * width), jnp.bfloat16),
            pltpu.VMEM((span, wide), jnp.bfloat16),
            pltpu.VMEM((wide, span), jnp.bfloat16),
            pltpu.VMEM((span, rows), jnp.float32),
            pltpu.VMEM((heads * rows, wide), jnp.bfloat16),
            pltpu.VMEM((heads * rows, LAT), jnp.bfloat16),
            pltpu.VMEM((span, heads * rows), jnp.bfloat16),
            pltpu.VMEM((span, heads * rows), jnp.bfloat16),
        ],
        compiler_params=pltpu.CompilerParams(vmem_limit_bytes=48 * 1024 * 1024),
        cost_estimate=pl.CostEstimate(
            flops=5_000_000_000, bytes_accessed=8_000_000, transcendentals=700_000
        ),
    )(place, advantage, segment, queries, rotated, cotangent, *key_blocks, mine, theirs)


def passed_along(value, steps):
    count = lax.axis_size("ctx")
    leading, last = (max(0, -steps), min(count, count - steps))
    return lax.ppermute(value, "ctx", [(source, source + steps) for source in range(leading, last)])


def on_device(q_nope, q_rope, latent, k_rope, d_out, advantage, segment, w_uk, w_uv):
    rows, width = q_nope.shape
    count = lax.axis_size("ctx")
    chips = count // 2
    reach = 4
    index = lax.axis_index("ctx")
    same_core = [[2 * chip + core for chip in range(chips)] for core in range(2)]
    swap = [(device, device ^ 1) for device in range(count)]

    up = jnp.concatenate([w_uk, w_uv], axis=1)
    mine = lax.all_to_all(
        jnp.broadcast_to(up[None], (chips,) + up.shape).reshape(chips * up.shape[0], up.shape[1]),
        "ctx",
        0,
        0,
        axis_index_groups=same_core,
        tiled=True,
    )
    theirs = lax.ppermute(mine, "ctx", swap)
    keys = jnp.concatenate([latent, k_rope], axis=1)
    blocks = [passed_along(keys, distance) for distance in range(reach, 0, -1)] + [keys]

    d_q_nope, d_q_rope, grad_earlier, grad_own, d_mine, d_theirs = layer(
        index.reshape(1),
        advantage.reshape(1, rows),
        segment.reshape(count, rows),
        q_nope,
        q_rope,
        d_out,
        blocks,
        mine,
        theirs,
    )

    total = grad_own
    for block in range(reach):
        piece = grad_earlier[block * rows : (block + 1) * rows]
        total = total + passed_along(piece, block - reach).astype(jnp.float32)
    heads_over = lax.axis_size("head")
    key_terms = lax.all_to_all(
        total.astype(jnp.bfloat16), "head", 0, 0, tiled=True
    ).reshape(heads_over, rows // heads_over, LAT + ROPE)
    d_keys = jnp.sum(key_terms.astype(jnp.float32), axis=0)

    arrived = lax.ppermute(d_theirs, "ctx", swap)
    chip_sum = (d_mine.astype(jnp.float32) + arrived.astype(jnp.float32)).astype(jnp.bfloat16)
    up_terms = lax.all_to_all(
        chip_sum, "ctx", 0, 0, axis_index_groups=same_core, tiled=True
    ).reshape(chips, LAT // count, 2 * width)
    d_up = jnp.sum(up_terms.astype(jnp.float32), axis=0)
    return (
        d_q_nope,
        d_q_rope,
        d_keys[:, :LAT],
        d_keys[:, LAT:],
        d_up[:, :width],
        d_up[:, width:],
    )


def solution(mesh):
    placed = (
        P("ctx", "head"),
        P("ctx", "head"),
        P("ctx", None),
        P("ctx", None),
        P("ctx", "head"),
        P("ctx"),
        P(),
        P("ctx", "head"),
        P("ctx", "head"),
    )
    return jax.shard_map(
        on_device,
        mesh=mesh,
        in_specs=placed,
        out_specs=(
            P("ctx", "head"),
            P("ctx", "head"),
            P(("ctx", "head"), None),
            P(("ctx", "head"), None),
            P("ctx", "head"),
            P("ctx", "head"),
        ),
        check_vma=False,
    )
```

```python
import functools
import math

import jax
import jax.numpy as jnp
from jax import lax
from jax.experimental import pallas as pl
from jax.experimental.pallas import tpu as pltpu
from jax.sharding import PartitionSpec as P

LAT = 512
ROPE = 64
NOPE = 128
VDIM = 128
FAR = -1e30


def dot_nt(left, right):
    return lax.dot_general(
        left, right, (((1,), (1,)), ((), ())), preferred_element_type=jnp.float32
    )


def dot_nn(left, right):
    return lax.dot_general(
        left, right, (((1,), (0,)), ((), ())), preferred_element_type=jnp.float32
    )


def dot_tn(left, right):
    return lax.dot_general(
        left, right, (((0,), (0,)), ((), ())), preferred_element_type=jnp.float32
    )


def column_of(row, count):
    return jnp.transpose(jnp.broadcast_to(row, (count, count)))


def layer_kernel(
    place,
    advantage,
    segment,
    queries_in,
    rotated_in,
    cotangent_in,
    keys_near,
    keys_far,
    weights_mine,
    weights_theirs,
    d_q_nope,
    d_q_rope,
    grad_kept,
    grad_given,
    grad_own,
    d_weights_mine,
    d_weights_theirs,
    queries,
    rotated,
    cotangent,
    weights,
    key_blocks,
    keys,
    keys_t,
    bias,
    absorbed,
    back_lat,
    probs_low,
    grad_score,
    d_weights,
    in_sems,
    out_sems,
):
    rows, width = queries.shape
    heads = width // NOPE
    span = keys.shape[0]
    reach = span // rows - 1
    ring = weights.shape[1]
    scale = 1.0 / math.sqrt(NOPE + ROPE)
    index = place[0]
    core = lax.rem(index, 2)

    loads = []

    def load(source, target):
        copy = pltpu.make_async_copy(source, target, in_sems.at[len(loads)])
        copy.start()
        loads.append(copy)

    load(keys_near, key_blocks.at[:, core])
    load(keys_far, key_blocks.at[:, 1 - core])
    key_loads = len(loads)
    load(queries_in, queries)
    load(cotangent_in, cotangent)
    load(rotated_in, rotated)
    for step in range(ring):
        load(weights_mine.at[step], weights.at[:, step, core])
        load(weights_theirs.at[step], weights.at[:, step, 1 - core])

    query_segment = segment[pl.ds(index, 1), :]
    query_at = lax.broadcasted_iota(jnp.int32, (rows, rows), 1)
    key_at = lax.broadcasted_iota(jnp.int32, (rows, rows), 0)
    for block in range(reach + 1):
        owner = index - (reach - block)
        key_row = segment[pl.ds(jnp.maximum(owner, 0), 1), :]
        key_segment = column_of(key_row, rows)
        allowed = (key_segment == query_segment) & (owner >= 0)
        if block == reach:
            allowed = allowed & (key_at <= query_at)
        bias[block * rows : (block + 1) * rows, :] = jnp.where(allowed, 0.0, FAR)
    advantage_column = column_of(advantage[...], rows)
    bias_pair = jnp.concatenate([bias[...], bias[...]], axis=1)

    for copy in loads[:key_loads]:
        copy.wait()
    for block in range(reach + 1):
        here = slice(block * rows, (block + 1) * rows)
        piece = key_blocks[(block + core) // 2, (block + core) % 2]
        keys[here, :] = piece
        keys_t[:, here] = jnp.transpose(piece)
    for copy in loads[key_loads:]:
        copy.wait()

    stores = []

    def store(source, target):
        copy = pltpu.make_async_copy(source, target, out_sems.at[len(stores)])
        copy.start()
        stores.append(copy)

    for pair in range(heads // 2):
        both = slice(pair * 2 * rows, (pair + 1) * 2 * rows)
        weighted = []
        for head in (2 * pair, 2 * pair + 1):
            here = slice(head * rows, (head + 1) * rows)
            nope = slice(head * NOPE, (head + 1) * NOPE)
            values = slice(width + head * VDIM, width + (head + 1) * VDIM)
            up_keys = weights[:, :, :, :, nope].reshape(LAT, NOPE)
            up_values = weights[:, :, :, :, values].reshape(LAT, VDIM)
            absorbed[here, :LAT] = dot_nt(queries[:, nope], up_keys).astype(jnp.bfloat16)
            absorbed[here, LAT:] = rotated[:, head * ROPE : (head + 1) * ROPE]
            weighted.append(
                (advantage_column * cotangent[:, nope].astype(jnp.float32)).astype(jnp.bfloat16)
            )
            back_lat[here, :] = dot_nt(weighted[-1], up_values).astype(jnp.bfloat16)
        scores = dot_nt(keys[...], absorbed[both, :]) * scale + bias_pair
        exponent = jnp.exp(scores - jnp.max(scores, axis=0, keepdims=True))
        probs = exponent * (1.0 / jnp.sum(exponent, axis=0, keepdims=True))
        low = probs.astype(jnp.bfloat16)
        probs_low[:, both] = low
        grad_prob = dot_nt(keys[:, :LAT], back_lat[both, :])
        row_delta = jnp.sum(probs * grad_prob, axis=0, keepdims=True)
        score = (probs * (grad_prob - row_delta) * scale).astype(jnp.bfloat16)
        grad_score[:, both] = score
        out_lat = dot_nn(keys_t[:LAT, :], low).astype(jnp.bfloat16)
        grad_abs = dot_nn(keys_t[...], score).astype(jnp.bfloat16)
        rope_rows = grad_abs[LAT:, :].astype(jnp.float32)
        rope_rows = jnp.concatenate([rope_rows[:, :rows], rope_rows[:, rows:]], axis=0)
        d_q_rope[:, pair * 2 * ROPE : (pair + 1) * 2 * ROPE] = jnp.transpose(rope_rows).astype(
            jnp.bfloat16
        )
        for side, head in enumerate((2 * pair, 2 * pair + 1)):
            nope = slice(head * NOPE, (head + 1) * NOPE)
            values = slice(width + head * VDIM, width + (head + 1) * VDIM)
            mine = slice(side * rows, (side + 1) * rows)
            up_keys = weights[:, :, :, :, nope].reshape(LAT, NOPE)
            d_q_nope[:, nope] = dot_tn(grad_abs[:LAT, mine], up_keys).astype(jnp.bfloat16)
            term_keys = dot_nn(grad_abs[:LAT, mine], queries[:, nope]).astype(jnp.bfloat16)
            term_values = dot_nn(out_lat[:, mine], weighted[side]).astype(jnp.bfloat16)
            shape = weights.shape[:4] + (NOPE,)
            d_weights[:, :, :, :, nope] = term_keys.reshape(shape)
            d_weights[:, :, :, :, values] = term_values.reshape(shape)
        if pair % 2 == 1:
            half = width // 2
            for start in (pair // 2 * half, width + pair // 2 * half):
                columns = pl.ds(start, half)
                for step in range(ring):
                    store(
                        d_weights.at[:, step, core, :, columns],
                        d_weights_mine.at[step, :, :, columns],
                    )
                    store(
                        d_weights.at[:, step, 1 - core, :, columns],
                        d_weights_theirs.at[step, :, :, columns],
                    )

    outs = (grad_kept.at[0], grad_given.at[0], grad_kept.at[1], grad_given.at[1], grad_own)
    for block, out in enumerate(outs):
        here = slice(block * rows, (block + 1) * rows)
        total = dot_nn(grad_score[here, :], absorbed[...])
        total_lat = total[:, :LAT] + dot_nn(probs_low[here, :], back_lat[...])
        out[:, :LAT] = total_lat.astype(out.dtype)
        out[:, LAT:] = total[:, LAT:].astype(out.dtype)
    for copy in stores:
        copy.wait()


def layer(place, advantage, segment, queries, rotated, cotangent, near, far, mine, theirs):
    rows, width = queries.shape
    heads = width // NOPE
    span = 5 * rows
    wide = LAT + ROPE
    whole = pl.BlockSpec(memory_space=pltpu.VMEM)
    apart = pl.BlockSpec(memory_space=pl.ANY)
    ring, steps = mine.shape[:2]
    parts = (steps, ring, 2, mine.shape[2], 2 * width)
    return pl.pallas_call(
        layer_kernel,
        out_shape=(
            jax.ShapeDtypeStruct((rows, width), jnp.bfloat16),
            jax.ShapeDtypeStruct((rows, heads * ROPE), jnp.bfloat16),
            jax.ShapeDtypeStruct((2, rows, wide), jnp.bfloat16),
            jax.ShapeDtypeStruct((2, rows, wide), jnp.bfloat16),
            jax.ShapeDtypeStruct((rows, wide), jnp.float32),
            jax.ShapeDtypeStruct(mine.shape, jnp.bfloat16),
            jax.ShapeDtypeStruct(theirs.shape, jnp.bfloat16),
        ),
        in_specs=[pl.BlockSpec(memory_space=pltpu.SMEM), whole, whole]
        + [apart] * 7,
        out_specs=(whole,) * 5 + (apart, apart),
        scratch_shapes=[
            pltpu.VMEM((rows, width), jnp.bfloat16),
            pltpu.VMEM((rows, heads * ROPE), jnp.bfloat16),
            pltpu.VMEM((rows, width), jnp.bfloat16),
            pltpu.VMEM(parts, jnp.bfloat16),
            pltpu.VMEM((3, 2, rows, wide), jnp.bfloat16),
            pltpu.VMEM((span, wide), jnp.bfloat16),
            pltpu.VMEM((wide, span), jnp.bfloat16),
            pltpu.VMEM((span, rows), jnp.float32),
            pltpu.VMEM((heads * rows, wide), jnp.bfloat16),
            pltpu.VMEM((heads * rows, LAT), jnp.bfloat16),
            pltpu.VMEM((span, heads * rows), jnp.bfloat16),
            pltpu.VMEM((span, heads * rows), jnp.bfloat16),
            pltpu.VMEM(parts, jnp.bfloat16),
            pltpu.SemaphoreType.DMA((5 + 2 * ring,)),
            pltpu.SemaphoreType.DMA((8 * ring,)),
        ],
        compiler_params=pltpu.CompilerParams(vmem_limit_bytes=56 * 1024 * 1024),
        cost_estimate=pl.CostEstimate(
            flops=5_000_000_000, bytes_accessed=8_000_000, transcendentals=700_000
        ),
    )(place, advantage, segment, queries, rotated, cotangent, near, far, mine, theirs)


def sum_kernel(shares, left, right):
    total = jnp.sum(shares[...].astype(jnp.float32), axis=0)
    left[...] = total[:, : left.shape[1]]
    right[...] = total[:, left.shape[1] :]


def summed(shares, cut):
    rows, width = shares.shape[1:]
    whole = pl.BlockSpec(memory_space=pltpu.VMEM)
    return pl.pallas_call(
        sum_kernel,
        out_shape=(
            jax.ShapeDtypeStruct((rows, cut), jnp.float32),
            jax.ShapeDtypeStruct((rows, width - cut), jnp.float32),
        ),
        in_specs=[whole],
        out_specs=(whole, whole),
        compiler_params=pltpu.CompilerParams(vmem_limit_bytes=8 * 1024 * 1024),
        cost_estimate=pl.CostEstimate(flops=1_000_000, bytes_accessed=500_000, transcendentals=0),
    )(shares)


def to_all(value, groups):
    spread = jnp.broadcast_to(value[None], (len(groups[0]),) + value.shape)
    return lax.all_to_all(spread, "ctx", 0, 0, axis_index_groups=groups, tiled=True)


def on_device(q_nope, q_rope, latent, k_rope, d_out, advantage, segment, w_uk, w_uv):
    rows, width = q_nope.shape
    count = lax.axis_size("ctx")
    ring = 4
    steps = count // (2 * ring)
    index = lax.axis_index("ctx")
    core = lax.rem(index, 2)
    place = index.reshape(1)

    def device(step, place, core):
        return (step * ring + place) * 2 + core

    along_y = [
        [device(step, place, core) for place in range(ring)]
        for step in range(steps)
        for core in range(2)
    ]
    along_z = [
        [device(step, place, core) for step in range(steps)]
        for place in range(ring)
        for core in range(2)
    ]

    def swapped(value):
        return lax.ppermute(value, "ctx", [(source, source ^ 1) for source in range(count)])

    def to_chip(value, chips):
        pairs = [(source, source + 2 * chips) for source in range(count)]
        return lax.ppermute(value, "ctx", [pair for pair in pairs if 0 <= pair[1] < count])

    up = jnp.concatenate([w_uk, w_uv], axis=1)
    column = to_all(up, along_z)
    keys = jnp.concatenate([latent, k_rope], axis=1)
    near = jnp.stack([to_chip(keys, 2), to_chip(keys, 1), keys])
    column, near = lax.optimization_barrier((column, near))
    mine = to_all(column, along_y)
    far = swapped(near)
    mine, near, far = lax.optimization_barrier((mine, near, far))
    theirs = swapped(mine)

    d_q_nope, d_q_rope, kept, given, own, d_mine, d_theirs = layer(
        place,
        advantage.reshape(1, rows),
        segment.reshape(count, rows),
        q_nope,
        q_rope,
        d_out,
        near,
        far,
        mine,
        theirs,
    )

    got = swapped(given).astype(jnp.float32)
    arrived = swapped(d_theirs)
    chip_sum = (d_mine.astype(jnp.float32) + arrived.astype(jnp.float32)).astype(jnp.bfloat16)
    far_sum = kept[0].astype(jnp.float32) + jnp.where(core == 1, got[0], 0.0)
    near_sum = kept[1].astype(jnp.float32) + jnp.where(core == 1, got[1], got[0])
    own_sum = own + jnp.where(core == 1, 0.0, got[1])
    far_sum = far_sum.astype(jnp.bfloat16)
    chip_sum, far_sum = lax.optimization_barrier((chip_sum, far_sum))
    shares = lax.all_to_all(chip_sum, "ctx", 0, 0, axis_index_groups=along_y, tiled=True)
    near_sum = (near_sum + to_chip(far_sum, -1).astype(jnp.float32)).astype(jnp.bfloat16)
    shares, near_sum = lax.optimization_barrier((shares, near_sum))
    d_column = jnp.sum(shares.astype(jnp.float32), axis=0).astype(jnp.bfloat16)
    d_shares = lax.all_to_all(d_column, "ctx", 0, 0, axis_index_groups=along_z, tiled=True)
    total = (own_sum + to_chip(near_sum, -1).astype(jnp.float32)).astype(jnp.bfloat16)
    d_shares, total = lax.optimization_barrier((d_shares, total))
    d_uk, d_uv = summed(d_shares, width)
    heads_over = lax.axis_size("head")
    key_terms = lax.all_to_all(total, "head", 0, 0, tiled=True)
    key_terms = key_terms.reshape(heads_over, rows // heads_over, LAT + ROPE)
    d_latent, d_k_rope = summed(key_terms, LAT)
    return (d_q_nope, d_q_rope, d_latent, d_k_rope, d_uk, d_uv)


def solution(mesh):
    placed = (
        P("ctx", "head"),
        P("ctx", "head"),
        P("ctx", None),
        P("ctx", None),
        P("ctx", "head"),
        P("ctx"),
        P(),
        P("ctx", "head"),
        P("ctx", "head"),
    )
    return jax.shard_map(
        on_device,
        mesh=mesh,
        in_specs=placed,
        out_specs=(
            P("ctx", "head"),
            P("ctx", "head"),
            P(("ctx", "head"), None),
            P(("ctx", "head"), None),
            P("ctx", "head"),
            P("ctx", "head"),
        ),
        check_vma=False,
    )
```

```python
import math

import jax
import jax.numpy as jnp
from jax import lax
from jax.experimental import pallas as pl
from jax.experimental.pallas import tpu as pltpu
from jax.sharding import PartitionSpec as P

LAT = 512
ROPE = 64
NOPE = 128
VDIM = 128
FAR = -1e30
MIB = 1024 * 1024


def dot_nt(left, right):
    return lax.dot_general(
        left, right, (((1,), (1,)), ((), ())), preferred_element_type=jnp.float32
    )


def dot_nn(left, right):
    return lax.dot_general(
        left, right, (((1,), (0,)), ((), ())), preferred_element_type=jnp.float32
    )


def dot_tn(left, right):
    return lax.dot_general(
        left, right, (((0,), (0,)), ((), ())), preferred_element_type=jnp.float32
    )


def column_of(row, count):
    return jnp.transpose(jnp.broadcast_to(row, (count, count)))


def split_kernel(place, advantage, queries, rotated, cotangent, kept, lent):
    rows, width = queries.shape
    half, rope_half = width // 2, rotated.shape[1] // 2
    core = lax.rem(place[0], 2)
    column = column_of(advantage[...], rows)[:, :1]
    for side, out in ((core, kept), (1 - core, lent)):
        here = pl.ds(pl.multiple_of(side * half, half), half)
        rope = pl.ds(pl.multiple_of(side * rope_half, rope_half), rope_half)
        out[:, :half] = queries[:, here]
        out[:, half:width] = (column * cotangent[:, here].astype(jnp.float32)).astype(jnp.bfloat16)
        out[:, width:] = rotated[:, rope]


def join_kernel(place, kept, returned, d_q_nope, d_q_rope):
    width, rope_width = d_q_nope.shape[1], d_q_rope.shape[1]
    half, rope_half = width // 2, rope_width // 2
    core = lax.rem(place[0], 2)
    for side, part in ((core, kept), (1 - core, returned)):
        here = pl.ds(pl.multiple_of(side * half, half), half)
        rope = pl.ds(pl.multiple_of(side * rope_half, rope_half), rope_half)
        d_q_nope[:, here] = part[:, :half]
        d_q_rope[:, rope] = part[:, half:]


def layer_kernel(
    place,
    segment,
    rows_kept,
    rows_lent,
    keys_near,
    keys_far,
    weights_in,
    d_rows_kept,
    d_rows_lent,
    grad_kept,
    grad_given,
    d_weights_out,
    tokens,
    weights,
    key_blocks,
    keys_t,
    bias,
    absorbed,
    back_lat,
    probs_low,
    grad_score,
    d_tokens,
    d_keys,
    d_weights,
    in_sems,
    out_sems,
):
    rows = tokens.shape[1]
    half = weights.shape[4] // 2
    heads = half // NOPE
    blocks = 2 * key_blocks.shape[0]
    span = (blocks - 1) * rows
    ring = weights.shape[1]
    scale = 1.0 / math.sqrt(NOPE + ROPE)
    core = lax.rem(place[0], 2)
    first = place[0] - core

    loads = []

    def load(source, target):
        copy = pltpu.make_async_copy(source, target, in_sems.at[len(loads)])
        copy.start()
        loads.append(copy)

    load(keys_near, key_blocks.at[:, core])
    load(keys_far, key_blocks.at[:, 1 - core])
    load(rows_kept, tokens.at[core])
    load(rows_lent, tokens.at[1 - core])
    for step in range(ring):
        load(weights_in.at[step], weights.at[:, step])

    query_at = lax.broadcasted_iota(jnp.int32, (rows, rows), 1)
    key_at = lax.broadcasted_iota(jnp.int32, (rows, rows), 0)
    query_segments = [segment[pl.ds(first + block, 1), :] for block in range(2)]
    for slot in range(blocks):
        owner = first - (blocks - 2) + slot
        key_row = segment[pl.ds(jnp.maximum(owner, 0), 1), :]
        key_segment = column_of(key_row, rows)
        for block in range(2):
            at = slot - block
            if not 0 <= at < blocks - 1:
                continue
            allowed = (key_segment == query_segments[block]) & (owner >= 0)
            if at == blocks - 2:
                allowed = allowed & (key_at <= query_at)
            bias[block, at * rows : (at + 1) * rows, :] = jnp.where(allowed, 0.0, FAR)

    loads[0].wait()
    loads[1].wait()
    for slot in range(blocks):
        here = slice(slot * rows, (slot + 1) * rows)
        keys_t[:, here] = jnp.transpose(key_blocks[slot // 2, slot % 2])
    for copy in loads[2:]:
        copy.wait()

    stores = []

    def store(source, target):
        copy = pltpu.make_async_copy(source, target, out_sems.at[len(stores)])
        copy.start()
        stores.append(copy)

    def head_weights(start):
        return weights[:, :, :, :, start : start + NOPE].reshape(LAT, NOPE)

    def keys_of(block, wide):
        return key_blocks[:, :, :, :wide].reshape(blocks * rows, wide)[
            block * rows : block * rows + span
        ]

    wide = LAT + ROPE
    units = [(pair, block) for pair in range(heads // 2) for block in range(2)]

    def columns_of(unit):
        pair, block = unit
        start = (block * heads + 2 * pair) * rows
        return slice(start, start + 2 * rows)

    def project(pair):
        for head in (2 * pair, 2 * pair + 1):
            nope = slice(head * NOPE, (head + 1) * NOPE)
            values = slice(half + head * VDIM, half + (head + 1) * VDIM)
            rope = slice(2 * half + head * ROPE, 2 * half + (head + 1) * ROPE)
            up = dot_nt(tokens[:, :, nope].reshape(2 * rows, NOPE), head_weights(nope.start))
            back = dot_nt(tokens[:, :, values].reshape(2 * rows, VDIM), head_weights(values.start))
            for block in range(2):
                here = slice((block * heads + head) * rows, (block * heads + head + 1) * rows)
                there = slice(block * rows, (block + 1) * rows)
                absorbed[here, :LAT] = up[there].astype(jnp.bfloat16)
                absorbed[here, LAT:] = tokens[block, :, rope]
                back_lat[here, :] = back[there].astype(jnp.bfloat16)

    def products(unit):
        here = columns_of(unit)
        scores = dot_nt(keys_of(unit[1], wide), absorbed[here, :])
        grad_prob = dot_nt(keys_of(unit[1], LAT), back_lat[here, :])
        return scores, grad_prob

    def soften(unit, scores, grad_prob):
        block = unit[1]
        mask = bias[block]
        scores = scores * scale + jnp.concatenate([mask, mask], axis=1)
        exponent = jnp.exp(scores - jnp.max(scores, axis=0, keepdims=True))
        probs = exponent * (1.0 / jnp.sum(exponent, axis=0, keepdims=True))
        low = probs.astype(jnp.bfloat16)
        row_delta = jnp.sum(probs * grad_prob, axis=0, keepdims=True)
        score = (probs * (grad_prob - row_delta) * scale).astype(jnp.bfloat16)
        here = columns_of(unit)
        probs_low[block * rows : block * rows + span, here] = low
        grad_score[block * rows : block * rows + span, here] = score
        there = slice(block * rows, block * rows + span)
        out_lat = dot_nn(keys_t[:LAT, there], low).astype(jnp.bfloat16)
        grad_abs = dot_nn(keys_t[:, there], score).astype(jnp.bfloat16)
        return out_lat, grad_abs

    def finish(pair, results):
        for block in range(2):
            rope_rows = results[block][1][LAT:, :].astype(jnp.float32)
            rope_rows = jnp.concatenate([rope_rows[:, :rows], rope_rows[:, rows:]], axis=0)
            start = half + 2 * pair * ROPE
            d_tokens[block, :, start : start + 2 * ROPE] = jnp.transpose(rope_rows).astype(
                jnp.bfloat16
            )
        for side, head in enumerate((2 * pair, 2 * pair + 1)):
            nope = slice(head * NOPE, (head + 1) * NOPE)
            values = slice(half + head * VDIM, half + (head + 1) * VDIM)
            mine = slice(side * rows, (side + 1) * rows)
            out_lat = jnp.concatenate([results[0][0][:, mine], results[1][0][:, mine]], axis=1)
            grad_abs = jnp.concatenate(
                [results[0][1][:LAT, mine], results[1][1][:LAT, mine]], axis=1
            )
            d_query = dot_tn(grad_abs, head_weights(nope.start)).astype(jnp.bfloat16)
            for block in range(2):
                d_tokens[block, :, nope] = d_query[block * rows : (block + 1) * rows]
            shape = weights.shape[:4] + (NOPE,)
            for columns, lead in ((nope, grad_abs), (values, out_lat)):
                term = dot_nn(lead, tokens[:, :, columns].reshape(2 * rows, NOPE))
                d_weights[:, :, :, :, columns] = term.astype(jnp.bfloat16).reshape(shape)
        for start in (2 * pair * NOPE, half + 2 * pair * VDIM):
            columns = pl.ds(start, 2 * NOPE)
            for step in range(ring):
                store(d_weights.at[:, step, :, :, columns], d_weights_out.at[step, :, :, :, columns])

    project(0)
    ahead = products(units[0])
    results = []
    for at, unit in enumerate(units):
        now = ahead
        if at + 1 < len(units):
            if units[at + 1][1] == 0:
                project(units[at + 1][0])
            ahead = products(units[at + 1])
        results.append(soften(unit, *now))
        if unit[1] == 1:
            finish(unit[0], results[-2:])
    store(d_tokens.at[core], d_rows_kept)
    store(d_tokens.at[1 - core], d_rows_lent)

    many = heads * rows
    for slot in range(blocks):
        here = slice(slot * rows, (slot + 1) * rows)
        low, high = (0, 2 * many)
        if slot == 0:
            high = many
        if slot == blocks - 1:
            low = many
        total = dot_nn(grad_score[here, low:high], absorbed[low:high, :])
        total_lat = total[:, :LAT] + dot_nn(probs_low[here, low:high], back_lat[low:high, :])
        d_keys[slot // 2, slot % 2, :, :LAT] = total_lat.astype(jnp.bfloat16)
        d_keys[slot // 2, slot % 2, :, LAT:] = total[:, LAT:].astype(jnp.bfloat16)
        if slot % 2 == 1:
            chip = slot // 2
            store(d_keys.at[chip, 1 - core], grad_given.at[chip])
            store(d_keys.at[chip, core], grad_kept.at[chip])
    for copy in stores:
        copy.wait()


WHOLE = pl.BlockSpec(memory_space=pltpu.VMEM)
SCALAR = pl.BlockSpec(memory_space=pltpu.SMEM)
APART = pl.BlockSpec(memory_space=pl.ANY)


def cost(flops, moved):
    return pl.CostEstimate(flops=flops, bytes_accessed=moved, transcendentals=0)


def layer(place, segment, kept, lent, near, far, weights):
    rows, packed = kept.shape
    chips, wide = near.shape[0], near.shape[2]
    ring, steps, cores, piece, width = weights.shape
    half = width // 2
    heads = half // NOPE
    span = (2 * chips - 1) * rows
    d_packed = half + heads * ROPE
    parts = (steps, ring, cores, piece, width)
    bf16 = jnp.bfloat16
    return pl.pallas_call(
        layer_kernel,
        out_shape=(
            jax.ShapeDtypeStruct((rows, d_packed), bf16),
            jax.ShapeDtypeStruct((rows, d_packed), bf16),
            jax.ShapeDtypeStruct(near.shape, bf16),
            jax.ShapeDtypeStruct(near.shape, bf16),
            jax.ShapeDtypeStruct(weights.shape, bf16),
        ),
        in_specs=[SCALAR, WHOLE] + [APART] * 5,
        out_specs=(APART,) * 5,
        scratch_shapes=[
            pltpu.VMEM((2, rows, packed), bf16),
            pltpu.VMEM(parts, bf16),
            pltpu.VMEM((chips, 2, rows, wide), bf16),
            pltpu.VMEM((wide, 2 * chips * rows), bf16),
            pltpu.VMEM((2, span, rows), jnp.float32),
            pltpu.VMEM((2 * heads * rows, wide), bf16),
            pltpu.VMEM((2 * heads * rows, LAT), bf16),
            pltpu.VMEM((2 * chips * rows, 2 * heads * rows), bf16),
            pltpu.VMEM((2 * chips * rows, 2 * heads * rows), bf16),
            pltpu.VMEM((2, rows, d_packed), bf16),
            pltpu.VMEM((chips, 2, rows, wide), bf16),
            pltpu.VMEM(parts, bf16),
            pltpu.SemaphoreType.DMA((4 + ring,)),
            pltpu.SemaphoreType.DMA((heads * ring + 2 + 2 * chips,)),
        ],
        compiler_params=pltpu.CompilerParams(vmem_limit_bytes=56 * MIB),
        cost_estimate=cost(5_000_000_000, 8_000_000),
    )(place, segment, kept, lent, near, far, weights)


def split_heads(place, advantage, queries, rotated, cotangent):
    rows, width = queries.shape
    packed = jax.ShapeDtypeStruct((rows, width + rotated.shape[1] // 2), jnp.bfloat16)
    return pl.pallas_call(
        split_kernel,
        out_shape=(packed, packed),
        in_specs=[SCALAR] + [WHOLE] * 4,
        out_specs=(WHOLE, WHOLE),
        compiler_params=pltpu.CompilerParams(vmem_limit_bytes=8 * MIB),
        cost_estimate=cost(1_000_000, 1_300_000),
    )(place, advantage, queries, rotated, cotangent)


def join_heads(place, kept, returned, width, rope_width):
    rows = kept.shape[0]
    return pl.pallas_call(
        join_kernel,
        out_shape=(
            jax.ShapeDtypeStruct((rows, width), jnp.bfloat16),
            jax.ShapeDtypeStruct((rows, rope_width), jnp.bfloat16),
        ),
        in_specs=[SCALAR, WHOLE, WHOLE],
        out_specs=(WHOLE, WHOLE),
        compiler_params=pltpu.CompilerParams(vmem_limit_bytes=8 * MIB),
        cost_estimate=cost(1_000_000, 800_000),
    )(place, kept, returned)


def key_sum_kernel(shares, left, right):
    total = jnp.sum(shares[...].astype(jnp.float32), axis=0)
    left[...] = total[:, : left.shape[1]]
    right[...] = total[:, left.shape[1] :]


def up_sum_kernel(shares, left, right):
    half = shares.shape[3] // 2
    for core in range(2):
        total = jnp.sum(shares[:, core].astype(jnp.float32), axis=0)
        left[:, core * half : (core + 1) * half] = total[:, :half]
        right[:, core * half : (core + 1) * half] = total[:, half:]


def summed(kernel, shares, rows, widths):
    return pl.pallas_call(
        kernel,
        out_shape=tuple(jax.ShapeDtypeStruct((rows, width), jnp.float32) for width in widths),
        in_specs=[WHOLE],
        out_specs=(WHOLE, WHOLE),
        compiler_params=pltpu.CompilerParams(vmem_limit_bytes=8 * MIB),
        cost_estimate=cost(1_000_000, 500_000),
    )(shares)


def on_device(q_nope, q_rope, latent, k_rope, d_out, advantage, segment, w_uk, w_uv):
    rows, width = q_nope.shape
    piece = w_uk.shape[0]
    half = width // 2
    count = lax.axis_size("ctx")
    ring = 4
    steps = count // (2 * ring)
    place = lax.axis_index("ctx").reshape(1)

    def device(step, place, core):
        return (step * ring + place) * 2 + core

    along_y = [
        [device(step, place, core) for place in range(ring)]
        for step in range(steps)
        for core in range(2)
    ]
    along_z = [
        [device(step, place, core) for step in range(steps) for core in range(2)]
        for place in range(ring)
    ]

    def swapped(value):
        return lax.ppermute(value, "ctx", [(source, source ^ 1) for source in range(count)])

    def to_chip(value, chips):
        pairs = [(source, source + 2 * chips) for source in range(count)]
        return lax.ppermute(value, "ctx", [pair for pair in pairs if 0 <= pair[1] < count])

    def exchanged(value, groups):
        return lax.all_to_all(value, "ctx", 0, 0, axis_index_groups=groups, tiled=True)

    up = jnp.stack([w_uk.reshape(piece, 2, half), w_uv.reshape(piece, 2, half)], axis=2)
    up = up.reshape(piece, 2, width).transpose(1, 0, 2)
    up = jnp.broadcast_to(up[None], (steps, 2, piece, width)).reshape(2 * steps, piece, width)
    column = exchanged(up, along_z)
    keys = jnp.concatenate([latent, k_rope], axis=1)
    near = jnp.stack([to_chip(keys, 2), to_chip(keys, 1), keys])
    column, near = lax.optimization_barrier((column, near))
    spread = jnp.broadcast_to(column[None], (ring,) + column.shape)
    weights = exchanged(spread, along_y).reshape(ring, steps, 2, piece, width)
    far = swapped(near)
    kept, lent = split_heads(place, advantage.reshape(1, rows), q_nope, q_rope, d_out)
    borrowed = swapped(lent)

    d_kept, d_lent, grad_kept, grad_given, d_weights = layer(
        place, segment.reshape(count, rows), kept, borrowed, near, far, weights
    )

    got = swapped(grad_given)
    sums = grad_kept.astype(jnp.float32) + got.astype(jnp.float32)
    far_sum = sums[0].astype(jnp.bfloat16)
    d_weights, far_sum = lax.optimization_barrier((d_weights, far_sum))
    shares = exchanged(d_weights, along_y)
    near_sum = (sums[1] + to_chip(far_sum, -1).astype(jnp.float32)).astype(jnp.bfloat16)
    returned = swapped(d_lent)
    d_q_nope, d_q_rope = join_heads(place, d_kept, returned, width, q_rope.shape[1])
    shares, near_sum, d_q_nope = lax.optimization_barrier((shares, near_sum, d_q_nope))
    d_column = jnp.sum(shares.astype(jnp.float32), axis=0).astype(jnp.bfloat16)
    d_shares = exchanged(d_column.reshape(2 * steps, piece, width), along_z)
    total = (sums[2] + to_chip(near_sum, -1).astype(jnp.float32)).astype(jnp.bfloat16)
    d_shares, total = lax.optimization_barrier((d_shares, total))
    d_uk, d_uv = summed(
        up_sum_kernel, d_shares.reshape(steps, 2, piece, width), piece, (width, width)
    )
    heads_over = lax.axis_size("head")
    key_terms = lax.all_to_all(total, "head", 0, 0, tiled=True)
    key_terms = key_terms.reshape(heads_over, rows // heads_over, LAT + ROPE)
    d_latent, d_k_rope = summed(key_sum_kernel, key_terms, rows // heads_over, (LAT, ROPE))
    return (d_q_nope, d_q_rope, d_latent, d_k_rope, d_uk, d_uv)


def solution(mesh):
    placed = (
        P("ctx", "head"),
        P("ctx", "head"),
        P("ctx", None),
        P("ctx", None),
        P("ctx", "head"),
        P("ctx"),
        P(),
        P("ctx", "head"),
        P("ctx", "head"),
    )
    return jax.shard_map(
        on_device,
        mesh=mesh,
        in_specs=placed,
        out_specs=(
            P("ctx", "head"),
            P("ctx", "head"),
            P(("ctx", "head"), None),
            P(("ctx", "head"), None),
            P("ctx", "head"),
            P("ctx", "head"),
        ),
        check_vma=False,
    )
```

```python
import math

import jax
import jax.numpy as jnp
from jax import lax
from jax.experimental import pallas as pl
from jax.experimental.pallas import tpu as pltpu
from jax.sharding import PartitionSpec as P

LAT = 512
ROPE = 64
NOPE = 128
VDIM = 128
FAR = -1e30
MIB = 1024 * 1024


def dot_nt(left, right):
    return lax.dot_general(
        left, right, (((1,), (1,)), ((), ())), preferred_element_type=jnp.float32
    )


def dot_nn(left, right):
    return lax.dot_general(
        left, right, (((1,), (0,)), ((), ())), preferred_element_type=jnp.float32
    )


def dot_tn(left, right):
    return lax.dot_general(
        left, right, (((0,), (0,)), ((), ())), preferred_element_type=jnp.float32
    )


def column_of(row, count):
    return jnp.transpose(jnp.broadcast_to(row, (count, count)))


def split_kernel(place, advantage, queries, rotated, cotangent, kept, lent):
    rows, width = queries.shape
    half, rope_half = width // 2, rotated.shape[1] // 2
    core = lax.rem(place[0], 2)
    column = column_of(advantage[...], rows)[:, :1]
    for side, out in ((core, kept), (1 - core, lent)):
        here = pl.ds(pl.multiple_of(side * half, half), half)
        rope = pl.ds(pl.multiple_of(side * rope_half, rope_half), rope_half)
        out[:, :half] = queries[:, here]
        out[:, half:width] = (column * cotangent[:, here].astype(jnp.float32)).astype(jnp.bfloat16)
        out[:, width:] = rotated[:, rope]


def join_kernel(place, kept, returned, d_q_nope, d_q_rope):
    width, rope_width = d_q_nope.shape[1], d_q_rope.shape[1]
    half, rope_half = width // 2, rope_width // 2
    core = lax.rem(place[0], 2)
    for side, part in ((core, kept), (1 - core, returned)):
        here = pl.ds(pl.multiple_of(side * half, half), half)
        rope = pl.ds(pl.multiple_of(side * rope_half, rope_half), rope_half)
        d_q_nope[:, here] = part[:, :half]
        d_q_rope[:, rope] = part[:, half:]


def layer_kernel(
    place,
    segment,
    rows_kept,
    rows_lent,
    keys_near,
    keys_far,
    weights_in,
    d_rows_kept,
    d_rows_lent,
    grad_kept,
    grad_given,
    d_weights_out,
    tokens,
    weights,
    key_blocks,
    keys_t,
    bias,
    absorbed,
    back_lat,
    probs_low,
    grad_score,
    d_tokens,
    d_keys,
    d_weights,
    in_sems,
    out_sems,
):
    rows = tokens.shape[1]
    half = weights.shape[4] // 2
    heads = half // NOPE
    blocks = 2 * key_blocks.shape[0]
    span = (blocks - 1) * rows
    ring = weights.shape[1]
    scale = 1.0 / math.sqrt(NOPE + ROPE)
    core = lax.rem(place[0], 2)
    first = place[0] - core

    loads = []

    def load(source, target):
        copy = pltpu.make_async_copy(source, target, in_sems.at[len(loads)])
        copy.start()
        loads.append(copy)

    load(keys_near, key_blocks.at[:, core])
    load(keys_far, key_blocks.at[:, 1 - core])
    load(rows_kept, tokens.at[core])
    load(rows_lent, tokens.at[1 - core])
    for step in range(ring):
        load(weights_in.at[step], weights.at[:, step])

    query_at = lax.broadcasted_iota(jnp.int32, (rows, rows), 1)
    key_at = lax.broadcasted_iota(jnp.int32, (rows, rows), 0)
    query_segments = [segment[pl.ds(first + block, 1), :] for block in range(2)]
    for slot in range(blocks):
        owner = first - (blocks - 2) + slot
        key_row = segment[pl.ds(jnp.maximum(owner, 0), 1), :]
        key_segment = column_of(key_row, rows)
        for block in range(2):
            at = slot - block
            if not 0 <= at < blocks - 1:
                continue
            allowed = (key_segment == query_segments[block]) & (owner >= 0)
            if at == blocks - 2:
                allowed = allowed & (key_at <= query_at)
            bias[block, at * rows : (at + 1) * rows, :] = jnp.where(allowed, 0.0, FAR)

    loads[0].wait()
    loads[1].wait()
    for slot in range(blocks):
        here = slice(slot * rows, (slot + 1) * rows)
        keys_t[:, here] = jnp.transpose(key_blocks[slot // 2, slot % 2])
    for copy in loads[2:]:
        copy.wait()

    stores = []

    def store(source, target):
        copy = pltpu.make_async_copy(source, target, out_sems.at[len(stores)])
        copy.start()
        stores.append(copy)

    def head_weights(start):
        return weights[:, :, :, :, start : start + NOPE].reshape(LAT, NOPE)

    def keys_of(block, wide):
        return key_blocks[:, :, :, :wide].reshape(blocks * rows, wide)[
            block * rows : block * rows + span
        ]

    wide = LAT + ROPE
    units = [(pair, block) for pair in range(heads // 2) for block in range(2)]

    def columns_of(unit):
        pair, block = unit
        start = (block * heads + 2 * pair) * rows
        return slice(start, start + 2 * rows)

    def project(pair):
        for head in (2 * pair, 2 * pair + 1):
            nope = slice(head * NOPE, (head + 1) * NOPE)
            values = slice(half + head * VDIM, half + (head + 1) * VDIM)
            rope = slice(2 * half + head * ROPE, 2 * half + (head + 1) * ROPE)
            up = dot_nt(tokens[:, :, nope].reshape(2 * rows, NOPE), head_weights(nope.start))
            back = dot_nt(tokens[:, :, values].reshape(2 * rows, VDIM), head_weights(values.start))
            for block in range(2):
                here = slice((block * heads + head) * rows, (block * heads + head + 1) * rows)
                there = slice(block * rows, (block + 1) * rows)
                absorbed[here, :LAT] = up[there].astype(jnp.bfloat16)
                absorbed[here, LAT:] = tokens[block, :, rope]
                back_lat[here, :] = back[there].astype(jnp.bfloat16)

    def products(unit):
        here = columns_of(unit)
        scores = dot_nt(keys_of(unit[1], wide), absorbed[here, :])
        grad_prob = dot_nt(keys_of(unit[1], LAT), back_lat[here, :])
        return scores, grad_prob

    def soften(unit, scores, grad_prob):
        block = unit[1]
        mask = bias[block]
        scores = scores * scale + jnp.concatenate([mask, mask], axis=1)
        exponent = jnp.exp(scores - jnp.max(scores, axis=0, keepdims=True))
        probs = exponent * (1.0 / jnp.sum(exponent, axis=0, keepdims=True))
        low = probs.astype(jnp.bfloat16)
        row_delta = jnp.sum(probs * grad_prob, axis=0, keepdims=True)
        score = (probs * (grad_prob - row_delta) * scale).astype(jnp.bfloat16)
        here = columns_of(unit)
        probs_low[block * rows : block * rows + span, here] = low
        grad_score[block * rows : block * rows + span, here] = score
        there = slice(block * rows, block * rows + span)
        out_lat = dot_nn(keys_t[:LAT, there], low).astype(jnp.bfloat16)
        grad_abs = dot_nn(keys_t[:, there], score).astype(jnp.bfloat16)
        return out_lat, grad_abs

    def finish(pair, results):
        for block in range(2):
            rope_rows = results[block][1][LAT:, :].astype(jnp.float32)
            rope_rows = jnp.concatenate([rope_rows[:, :rows], rope_rows[:, rows:]], axis=0)
            start = half + 2 * pair * ROPE
            d_tokens[block, :, start : start + 2 * ROPE] = jnp.transpose(rope_rows).astype(
                jnp.bfloat16
            )
        for side, head in enumerate((2 * pair, 2 * pair + 1)):
            nope = slice(head * NOPE, (head + 1) * NOPE)
            values = slice(half + head * VDIM, half + (head + 1) * VDIM)
            mine = slice(side * rows, (side + 1) * rows)
            out_lat = jnp.concatenate([results[0][0][:, mine], results[1][0][:, mine]], axis=1)
            grad_abs = jnp.concatenate(
                [results[0][1][:LAT, mine], results[1][1][:LAT, mine]], axis=1
            )
            d_query = dot_tn(grad_abs, head_weights(nope.start)).astype(jnp.bfloat16)
            for block in range(2):
                d_tokens[block, :, nope] = d_query[block * rows : (block + 1) * rows]
            shape = weights.shape[:4] + (NOPE,)
            for columns, lead in ((nope, grad_abs), (values, out_lat)):
                term = dot_nn(lead, tokens[:, :, columns].reshape(2 * rows, NOPE))
                d_weights[:, :, :, :, columns] = term.astype(jnp.bfloat16).reshape(shape)
        for start in (2 * pair * NOPE, half + 2 * pair * VDIM):
            columns = pl.ds(start, 2 * NOPE)
            for step in range(ring):
                store(d_weights.at[:, step, :, :, columns], d_weights_out.at[step, :, :, :, columns])

    project(0)
    ahead = products(units[0])
    results = []
    for at, unit in enumerate(units):
        now = ahead
        if at + 1 < len(units):
            if units[at + 1][1] == 0:
                project(units[at + 1][0])
            ahead = products(units[at + 1])
        results.append(soften(unit, *now))
        if unit[1] == 1:
            finish(unit[0], results[-2:])
    store(d_tokens.at[core], d_rows_kept)
    store(d_tokens.at[1 - core], d_rows_lent)

    many = heads * rows
    for slot in range(blocks):
        here = slice(slot * rows, (slot + 1) * rows)
        low, high = (0, 2 * many)
        if slot == 0:
            high = many
        if slot == blocks - 1:
            low = many
        total = dot_nn(grad_score[here, low:high], absorbed[low:high, :])
        total_lat = total[:, :LAT] + dot_nn(probs_low[here, low:high], back_lat[low:high, :])
        d_keys[slot // 2, slot % 2, :, :LAT] = total_lat.astype(jnp.bfloat16)
        d_keys[slot // 2, slot % 2, :, LAT:] = total[:, LAT:].astype(jnp.bfloat16)
        if slot % 2 == 1:
            chip = slot // 2
            store(d_keys.at[chip, 1 - core], grad_given.at[chip])
            store(d_keys.at[chip, core], grad_kept.at[chip])
    for copy in stores:
        copy.wait()


WHOLE = pl.BlockSpec(memory_space=pltpu.VMEM)
SCALAR = pl.BlockSpec(memory_space=pltpu.SMEM)
APART = pl.BlockSpec(memory_space=pl.ANY)


def cost(flops, moved):
    return pl.CostEstimate(flops=flops, bytes_accessed=moved, transcendentals=0)


def layer(place, segment, kept, lent, near, far, weights):
    rows, packed = kept.shape
    chips, wide = near.shape[0], near.shape[2]
    ring, steps, cores, piece, width = weights.shape
    half = width // 2
    heads = half // NOPE
    span = (2 * chips - 1) * rows
    d_packed = half + heads * ROPE
    parts = (steps, ring, cores, piece, width)
    bf16 = jnp.bfloat16
    return pl.pallas_call(
        layer_kernel,
        out_shape=(
            jax.ShapeDtypeStruct((rows, d_packed), bf16),
            jax.ShapeDtypeStruct((rows, d_packed), bf16),
            jax.ShapeDtypeStruct(near.shape, bf16),
            jax.ShapeDtypeStruct(near.shape, bf16),
            jax.ShapeDtypeStruct(weights.shape, bf16),
        ),
        in_specs=[SCALAR, WHOLE] + [APART] * 5,
        out_specs=(APART,) * 5,
        scratch_shapes=[
            pltpu.VMEM((2, rows, packed), bf16),
            pltpu.VMEM(parts, bf16),
            pltpu.VMEM((chips, 2, rows, wide), bf16),
            pltpu.VMEM((wide, 2 * chips * rows), bf16),
            pltpu.VMEM((2, span, rows), jnp.float32),
            pltpu.VMEM((2 * heads * rows, wide), bf16),
            pltpu.VMEM((2 * heads * rows, LAT), bf16),
            pltpu.VMEM((2 * chips * rows, 2 * heads * rows), bf16),
            pltpu.VMEM((2 * chips * rows, 2 * heads * rows), bf16),
            pltpu.VMEM((2, rows, d_packed), bf16),
            pltpu.VMEM((chips, 2, rows, wide), bf16),
            pltpu.VMEM(parts, bf16),
            pltpu.SemaphoreType.DMA((4 + ring,)),
            pltpu.SemaphoreType.DMA((heads * ring + 2 + 2 * chips,)),
        ],
        compiler_params=pltpu.CompilerParams(vmem_limit_bytes=56 * MIB),
        cost_estimate=cost(5_000_000_000, 8_000_000),
    )(place, segment, kept, lent, near, far, weights)


def split_heads(place, advantage, queries, rotated, cotangent):
    rows, width = queries.shape
    packed = jax.ShapeDtypeStruct((rows, width + rotated.shape[1] // 2), jnp.bfloat16)
    return pl.pallas_call(
        split_kernel,
        out_shape=(packed, packed),
        in_specs=[SCALAR] + [WHOLE] * 4,
        out_specs=(WHOLE, WHOLE),
        compiler_params=pltpu.CompilerParams(vmem_limit_bytes=8 * MIB),
        cost_estimate=cost(1_000_000, 1_300_000),
    )(place, advantage, queries, rotated, cotangent)


def join_heads(place, kept, returned, width, rope_width):
    rows = kept.shape[0]
    return pl.pallas_call(
        join_kernel,
        out_shape=(
            jax.ShapeDtypeStruct((rows, width), jnp.bfloat16),
            jax.ShapeDtypeStruct((rows, rope_width), jnp.bfloat16),
        ),
        in_specs=[SCALAR, WHOLE, WHOLE],
        out_specs=(WHOLE, WHOLE),
        compiler_params=pltpu.CompilerParams(vmem_limit_bytes=8 * MIB),
        cost_estimate=cost(1_000_000, 800_000),
    )(place, kept, returned)


def slot_kernel(left, right, out, sems):
    half = left.shape[1] // 2
    copies = []
    for slot in range(out.shape[0]):
        here = pl.ds(slot % 2 * half, half)
        for at, part in enumerate((left, right)):
            target = out.at[slot, :, pl.ds(at * half, half)]
            copies.append(pltpu.make_async_copy(part.at[:, here], target, sems.at[slot, at]))
            copies[-1].start()
    for copy in copies:
        copy.wait()


def slots(left, right, count):
    return pl.pallas_call(
        slot_kernel,
        out_shape=jax.ShapeDtypeStruct((count,) + left.shape, left.dtype),
        in_specs=[APART, APART],
        out_specs=WHOLE,
        scratch_shapes=[pltpu.SemaphoreType.DMA((count, 2))],
        compiler_params=pltpu.CompilerParams(vmem_limit_bytes=56 * MIB),
        cost_estimate=cost(100_000, 300_000),
    )(left, right)


def key_sum_kernel(shares, left, right):
    total = jnp.sum(shares[...].astype(jnp.float32), axis=0)
    left[...] = total[:, : left.shape[1]]
    right[...] = total[:, left.shape[1] :]


def up_sum_kernel(shares, left, right):
    half = shares.shape[3] // 2
    for core in range(2):
        total = jnp.sum(shares[:, core].astype(jnp.float32), axis=0)
        left[:, core * half : (core + 1) * half] = total[:, :half]
        right[:, core * half : (core + 1) * half] = total[:, half:]


def summed(kernel, shares, rows, widths):
    return pl.pallas_call(
        kernel,
        out_shape=tuple(jax.ShapeDtypeStruct((rows, width), jnp.float32) for width in widths),
        in_specs=[WHOLE],
        out_specs=(WHOLE, WHOLE),
        compiler_params=pltpu.CompilerParams(vmem_limit_bytes=8 * MIB),
        cost_estimate=cost(1_000_000, 500_000),
    )(shares)


def on_device(q_nope, q_rope, latent, k_rope, d_out, advantage, segment, w_uk, w_uv):
    rows, width = q_nope.shape
    piece = w_uk.shape[0]
    count = lax.axis_size("ctx")
    ring = 4
    steps = count // (2 * ring)
    place = lax.axis_index("ctx").reshape(1)

    def device(step, place, core):
        return (step * ring + place) * 2 + core

    along_y = [
        [device(step, place, core) for place in range(ring)]
        for step in range(steps)
        for core in range(2)
    ]
    along_z = [
        [device(step, place, core) for step in range(steps) for core in range(2)]
        for place in range(ring)
    ]

    def swapped(value):
        return lax.ppermute(value, "ctx", [(source, source ^ 1) for source in range(count)])

    def to_chip(value, chips):
        pairs = [(source, source + 2 * chips) for source in range(count)]
        return lax.ppermute(value, "ctx", [pair for pair in pairs if 0 <= pair[1] < count])

    def exchanged(value, groups):
        return lax.all_to_all(value, "ctx", 0, 0, axis_index_groups=groups, tiled=True)

    column = exchanged(slots(w_uk, w_uv, 2 * steps), along_z)
    keys = jnp.concatenate([latent, k_rope], axis=1)
    near = jnp.stack([to_chip(keys, 2), to_chip(keys, 1), keys])
    column, near = lax.optimization_barrier((column, near))
    spread = jnp.broadcast_to(column[None], (ring,) + column.shape)
    weights = exchanged(spread, along_y).reshape(ring, steps, 2, piece, width)
    far = swapped(near)
    kept, lent = split_heads(place, advantage.reshape(1, rows), q_nope, q_rope, d_out)
    borrowed = swapped(lent)

    d_kept, d_lent, grad_kept, grad_given, d_weights = layer(
        place, segment.reshape(count, rows), kept, borrowed, near, far, weights
    )

    got = swapped(grad_given)
    sums = grad_kept.astype(jnp.float32) + got.astype(jnp.float32)
    far_sum = sums[0].astype(jnp.bfloat16)
    shares = exchanged(d_weights, along_y)
    near_sum = (sums[1] + to_chip(far_sum, -1).astype(jnp.float32)).astype(jnp.bfloat16)
    shares, near_sum = lax.optimization_barrier((shares, near_sum))
    d_column = jnp.sum(shares.astype(jnp.float32), axis=0).astype(jnp.bfloat16)
    d_shares = exchanged(d_column.reshape(2 * steps, piece, width), along_z)
    total = (sums[2] + to_chip(near_sum, -1).astype(jnp.float32)).astype(jnp.bfloat16)
    returned = swapped(d_lent)
    d_q_nope, d_q_rope = join_heads(place, d_kept, returned, width, q_rope.shape[1])
    d_shares, total, d_q_nope = lax.optimization_barrier((d_shares, total, d_q_nope))
    d_uk, d_uv = summed(
        up_sum_kernel, d_shares.reshape(steps, 2, piece, width), piece, (width, width)
    )
    heads_over = lax.axis_size("head")
    key_terms = lax.all_to_all(total, "head", 0, 0, tiled=True)
    key_terms = key_terms.reshape(heads_over, rows // heads_over, LAT + ROPE)
    d_latent, d_k_rope = summed(key_sum_kernel, key_terms, rows // heads_over, (LAT, ROPE))
    return (d_q_nope, d_q_rope, d_latent, d_k_rope, d_uk, d_uv)


def solution(mesh):
    placed = (
        P("ctx", "head"),
        P("ctx", "head"),
        P("ctx", None),
        P("ctx", None),
        P("ctx", "head"),
        P("ctx"),
        P(),
        P("ctx", "head"),
        P("ctx", "head"),
    )
    return jax.shard_map(
        on_device,
        mesh=mesh,
        in_specs=placed,
        out_specs=(
            P("ctx", "head"),
            P("ctx", "head"),
            P(("ctx", "head"), None),
            P(("ctx", "head"), None),
            P("ctx", "head"),
            P("ctx", "head"),
        ),
        check_vma=False,
    )
```

```python
import math

import jax
import jax.numpy as jnp
from jax import lax
from jax.experimental import pallas as pl
from jax.experimental.pallas import tpu as pltpu
from jax.sharding import PartitionSpec as P

LAT = 512
ROPE = 64
NOPE = 128
VDIM = 128
FAR = -1e30
MIB = 1024 * 1024


def dot_nt(left, right):
    return lax.dot_general(
        left, right, (((1,), (1,)), ((), ())), preferred_element_type=jnp.float32
    )


def dot_nn(left, right):
    return lax.dot_general(
        left, right, (((1,), (0,)), ((), ())), preferred_element_type=jnp.float32
    )


def dot_tn(left, right):
    return lax.dot_general(
        left, right, (((0,), (0,)), ((), ())), preferred_element_type=jnp.float32
    )


def column_of(row, count):
    return jnp.transpose(jnp.broadcast_to(row, (count, count)))


def split_kernel(place, advantage, queries, rotated, cotangent, kept, lent):
    rows, width = queries.shape
    half, rope_half = width // 2, rotated.shape[1] // 2
    core = lax.rem(place[0], 2)
    column = column_of(advantage[...], rows)[:, :1]
    for side, out in ((core, kept), (1 - core, lent)):
        here = pl.ds(pl.multiple_of(side * half, half), half)
        rope = pl.ds(pl.multiple_of(side * rope_half, rope_half), rope_half)
        out[:, :half] = queries[:, here]
        out[:, half:width] = (column * cotangent[:, here].astype(jnp.float32)).astype(jnp.bfloat16)
        out[:, width:] = rotated[:, rope]


def join_kernel(place, kept, returned, d_q_nope, d_q_rope):
    width, rope_width = d_q_nope.shape[1], d_q_rope.shape[1]
    half, rope_half = width // 2, rope_width // 2
    core = lax.rem(place[0], 2)
    for side, part in ((core, kept), (1 - core, returned)):
        here = pl.ds(pl.multiple_of(side * half, half), half)
        rope = pl.ds(pl.multiple_of(side * rope_half, rope_half), rope_half)
        d_q_nope[:, here] = part[:, :half]
        d_q_rope[:, rope] = part[:, half:]


def layer_kernel(
    place,
    segment,
    rows_kept,
    rows_lent,
    keys_near,
    keys_far,
    weights_in,
    d_rows_kept,
    d_rows_lent,
    grad_kept,
    grad_given,
    d_weights_out,
    tokens,
    weights,
    key_blocks,
    keys_t,
    bias,
    absorbed,
    back_lat,
    probs_low,
    grad_score,
    d_tokens,
    d_keys,
    d_weights,
    in_sems,
    out_sems,
):
    rows = tokens.shape[1]
    half = weights.shape[4] // 2
    heads = half // NOPE
    blocks = 2 * key_blocks.shape[0]
    span = (blocks - 1) * rows
    ring = weights.shape[1]
    scale = 1.0 / math.sqrt(NOPE + ROPE)
    core = lax.rem(place[0], 2)
    first = place[0] - core

    loads = []

    def load(source, target):
        copy = pltpu.make_async_copy(source, target, in_sems.at[len(loads)])
        copy.start()
        loads.append(copy)

    load(keys_near, key_blocks.at[:, core])
    load(keys_far, key_blocks.at[:, 1 - core])
    load(rows_kept, tokens.at[core])
    load(rows_lent, tokens.at[1 - core])
    for step in range(ring):
        load(weights_in.at[step], weights.at[:, step])

    query_at = lax.broadcasted_iota(jnp.int32, (rows, rows), 1)
    key_at = lax.broadcasted_iota(jnp.int32, (rows, rows), 0)
    query_segments = [segment[pl.ds(first + block, 1), :] for block in range(2)]
    for slot in range(blocks):
        owner = first - (blocks - 2) + slot
        key_row = segment[pl.ds(jnp.maximum(owner, 0), 1), :]
        key_segment = column_of(key_row, rows)
        for block in range(2):
            at = slot - block
            if not 0 <= at < blocks - 1:
                continue
            allowed = (key_segment == query_segments[block]) & (owner >= 0)
            if at == blocks - 2:
                allowed = allowed & (key_at <= query_at)
            bias[block, at * rows : (at + 1) * rows, :] = jnp.where(allowed, 0.0, FAR)

    loads[0].wait()
    loads[1].wait()
    for slot in range(blocks):
        here = slice(slot * rows, (slot + 1) * rows)
        keys_t[:, here] = jnp.transpose(key_blocks[slot // 2, slot % 2])
    for copy in loads[2:]:
        copy.wait()

    stores = []

    def store(source, target):
        copy = pltpu.make_async_copy(source, target, out_sems.at[len(stores)])
        copy.start()
        stores.append(copy)

    def head_weights(start):
        return weights[:, :, :, :, start : start + NOPE].reshape(LAT, NOPE)

    def keys_of(block, wide):
        return key_blocks[:, :, :, :wide].reshape(blocks * rows, wide)[
            block * rows : block * rows + span
        ]

    wide = LAT + ROPE
    units = [(pair, block) for pair in range(heads // 2) for block in range(2)]

    def columns_of(unit):
        pair, block = unit
        start = (block * heads + 2 * pair) * rows
        return slice(start, start + 2 * rows)

    def project(pair):
        for head in (2 * pair, 2 * pair + 1):
            nope = slice(head * NOPE, (head + 1) * NOPE)
            values = slice(half + head * VDIM, half + (head + 1) * VDIM)
            rope = slice(2 * half + head * ROPE, 2 * half + (head + 1) * ROPE)
            up = dot_nt(tokens[:, :, nope].reshape(2 * rows, NOPE), head_weights(nope.start))
            back = dot_nt(tokens[:, :, values].reshape(2 * rows, VDIM), head_weights(values.start))
            for block in range(2):
                here = slice((block * heads + head) * rows, (block * heads + head + 1) * rows)
                there = slice(block * rows, (block + 1) * rows)
                absorbed[here, :LAT] = up[there].astype(jnp.bfloat16)
                absorbed[here, LAT:] = tokens[block, :, rope]
                back_lat[here, :] = back[there].astype(jnp.bfloat16)

    def products(unit):
        here = columns_of(unit)
        scores = dot_nt(keys_of(unit[1], wide), absorbed[here, :])
        grad_prob = dot_nt(keys_of(unit[1], LAT), back_lat[here, :])
        return scores, grad_prob

    def soften(unit, scores, grad_prob):
        block = unit[1]
        mask = bias[block]
        scores = scores * scale + jnp.concatenate([mask, mask], axis=1)
        exponent = jnp.exp(scores - jnp.max(scores, axis=0, keepdims=True))
        probs = exponent * (1.0 / jnp.sum(exponent, axis=0, keepdims=True))
        low = probs.astype(jnp.bfloat16)
        row_delta = jnp.sum(probs * grad_prob, axis=0, keepdims=True)
        score = (probs * (grad_prob - row_delta) * scale).astype(jnp.bfloat16)
        here = columns_of(unit)
        probs_low[block * rows : block * rows + span, here] = low
        grad_score[block * rows : block * rows + span, here] = score
        there = slice(block * rows, block * rows + span)
        out_lat = dot_nn(keys_t[:LAT, there], low).astype(jnp.bfloat16)
        grad_abs = dot_nn(keys_t[:, there], score).astype(jnp.bfloat16)
        return out_lat, grad_abs

    def finish(pair, results):
        for block in range(2):
            rope_rows = results[block][1][LAT:, :].astype(jnp.float32)
            rope_rows = jnp.concatenate([rope_rows[:, :rows], rope_rows[:, rows:]], axis=0)
            start = half + 2 * pair * ROPE
            d_tokens[block, :, start : start + 2 * ROPE] = jnp.transpose(rope_rows).astype(
                jnp.bfloat16
            )
        for side, head in enumerate((2 * pair, 2 * pair + 1)):
            nope = slice(head * NOPE, (head + 1) * NOPE)
            values = slice(half + head * VDIM, half + (head + 1) * VDIM)
            mine = slice(side * rows, (side + 1) * rows)
            out_lat = jnp.concatenate([results[0][0][:, mine], results[1][0][:, mine]], axis=1)
            grad_abs = jnp.concatenate(
                [results[0][1][:LAT, mine], results[1][1][:LAT, mine]], axis=1
            )
            d_query = dot_tn(grad_abs, head_weights(nope.start)).astype(jnp.bfloat16)
            for block in range(2):
                d_tokens[block, :, nope] = d_query[block * rows : (block + 1) * rows]
            shape = weights.shape[:4] + (NOPE,)
            for columns, lead in ((nope, grad_abs), (values, out_lat)):
                term = dot_nn(lead, tokens[:, :, columns].reshape(2 * rows, NOPE))
                d_weights[:, :, :, :, columns] = term.astype(jnp.bfloat16).reshape(shape)
        for start in (2 * pair * NOPE, half + 2 * pair * VDIM):
            columns = pl.ds(start, 2 * NOPE)
            for step in range(ring):
                store(d_weights.at[:, step, :, :, columns], d_weights_out.at[step, :, :, :, columns])

    project(0)
    ahead = products(units[0])
    results = []
    for at, unit in enumerate(units):
        now = ahead
        if at + 1 < len(units):
            if units[at + 1][1] == 0:
                project(units[at + 1][0])
            ahead = products(units[at + 1])
        results.append(soften(unit, *now))
        if unit[1] == 1:
            finish(unit[0], results[-2:])
    store(d_tokens.at[core], d_rows_kept)
    store(d_tokens.at[1 - core], d_rows_lent)

    many = heads * rows
    for slot in range(blocks):
        here = slice(slot * rows, (slot + 1) * rows)
        low, high = (0, 2 * many)
        if slot == 0:
            high = many
        if slot == blocks - 1:
            low = many
        total = dot_nn(grad_score[here, low:high], absorbed[low:high, :])
        total_lat = total[:, :LAT] + dot_nn(probs_low[here, low:high], back_lat[low:high, :])
        d_keys[slot // 2, slot % 2, :, :LAT] = total_lat.astype(jnp.bfloat16)
        d_keys[slot // 2, slot % 2, :, LAT:] = total[:, LAT:].astype(jnp.bfloat16)
        if slot % 2 == 1:
            chip = slot // 2
            store(d_keys.at[chip, 1 - core], grad_given.at[chip])
            store(d_keys.at[chip, core], grad_kept.at[chip])
    for copy in stores:
        copy.wait()


WHOLE = pl.BlockSpec(memory_space=pltpu.VMEM)
SCALAR = pl.BlockSpec(memory_space=pltpu.SMEM)
APART = pl.BlockSpec(memory_space=pl.ANY)


def cost(flops, moved):
    return pl.CostEstimate(flops=flops, bytes_accessed=moved, transcendentals=0)


def layer(place, segment, kept, lent, near, far, weights):
    rows, packed = kept.shape
    chips, wide = near.shape[0], near.shape[2]
    ring, steps, cores, piece, width = weights.shape
    half = width // 2
    heads = half // NOPE
    span = (2 * chips - 1) * rows
    d_packed = half + heads * ROPE
    parts = (steps, ring, cores, piece, width)
    bf16 = jnp.bfloat16
    return pl.pallas_call(
        layer_kernel,
        out_shape=(
            jax.ShapeDtypeStruct((rows, d_packed), bf16),
            jax.ShapeDtypeStruct((rows, d_packed), bf16),
            jax.ShapeDtypeStruct(near.shape, bf16),
            jax.ShapeDtypeStruct(near.shape, bf16),
            jax.ShapeDtypeStruct(weights.shape, bf16),
        ),
        in_specs=[SCALAR, WHOLE] + [APART] * 5,
        out_specs=(APART,) * 5,
        scratch_shapes=[
            pltpu.VMEM((2, rows, packed), bf16),
            pltpu.VMEM(parts, bf16),
            pltpu.VMEM((chips, 2, rows, wide), bf16),
            pltpu.VMEM((wide, 2 * chips * rows), bf16),
            pltpu.VMEM((2, span, rows), jnp.float32),
            pltpu.VMEM((2 * heads * rows, wide), bf16),
            pltpu.VMEM((2 * heads * rows, LAT), bf16),
            pltpu.VMEM((2 * chips * rows, 2 * heads * rows), bf16),
            pltpu.VMEM((2 * chips * rows, 2 * heads * rows), bf16),
            pltpu.VMEM((2, rows, d_packed), bf16),
            pltpu.VMEM((chips, 2, rows, wide), bf16),
            pltpu.VMEM(parts, bf16),
            pltpu.SemaphoreType.DMA((4 + ring,)),
            pltpu.SemaphoreType.DMA((heads * ring + 2 + 2 * chips,)),
        ],
        compiler_params=pltpu.CompilerParams(vmem_limit_bytes=56 * MIB),
        cost_estimate=cost(5_000_000_000, 8_000_000),
    )(place, segment, kept, lent, near, far, weights)


def split_heads(place, advantage, queries, rotated, cotangent):
    rows, width = queries.shape
    packed = jax.ShapeDtypeStruct((rows, width + rotated.shape[1] // 2), jnp.bfloat16)
    return pl.pallas_call(
        split_kernel,
        out_shape=(packed, packed),
        in_specs=[SCALAR] + [WHOLE] * 4,
        out_specs=(WHOLE, WHOLE),
        compiler_params=pltpu.CompilerParams(vmem_limit_bytes=8 * MIB),
        cost_estimate=cost(1_000_000, 1_300_000),
    )(place, advantage, queries, rotated, cotangent)


def join_heads(place, kept, returned, width, rope_width):
    rows = kept.shape[0]
    return pl.pallas_call(
        join_kernel,
        out_shape=(
            jax.ShapeDtypeStruct((rows, width), jnp.bfloat16),
            jax.ShapeDtypeStruct((rows, rope_width), jnp.bfloat16),
        ),
        in_specs=[SCALAR, WHOLE, WHOLE],
        out_specs=(WHOLE, WHOLE),
        compiler_params=pltpu.CompilerParams(vmem_limit_bytes=8 * MIB),
        cost_estimate=cost(1_000_000, 800_000),
    )(place, kept, returned)


def slot_kernel(left, right, out, sems):
    half = left.shape[1] // 2
    copies = []
    for slot in range(out.shape[0]):
        here = pl.ds(slot % 2 * half, half)
        for at, part in enumerate((left, right)):
            target = out.at[slot, :, pl.ds(at * half, half)]
            copies.append(pltpu.make_async_copy(part.at[:, here], target, sems.at[slot, at]))
            copies[-1].start()
    for copy in copies:
        copy.wait()


def slots(left, right, count):
    return pl.pallas_call(
        slot_kernel,
        out_shape=jax.ShapeDtypeStruct((count,) + left.shape, left.dtype),
        in_specs=[APART, APART],
        out_specs=WHOLE,
        scratch_shapes=[pltpu.SemaphoreType.DMA((count, 2))],
        compiler_params=pltpu.CompilerParams(vmem_limit_bytes=56 * MIB),
        cost_estimate=cost(100_000, 300_000),
    )(left, right)


def key_sum_kernel(shares, left, right):
    total = jnp.sum(shares[...].astype(jnp.float32), axis=0)
    left[...] = total[:, : left.shape[1]]
    right[...] = total[:, left.shape[1] :]


def up_sum_kernel(shares, left, right):
    half = shares.shape[3] // 2
    for core in range(2):
        total = jnp.sum(shares[:, core].astype(jnp.float32), axis=0)
        left[:, core * half : (core + 1) * half] = total[:, :half]
        right[:, core * half : (core + 1) * half] = total[:, half:]


def summed(kernel, shares, rows, widths):
    return pl.pallas_call(
        kernel,
        out_shape=tuple(jax.ShapeDtypeStruct((rows, width), jnp.float32) for width in widths),
        in_specs=[WHOLE],
        out_specs=(WHOLE, WHOLE),
        compiler_params=pltpu.CompilerParams(vmem_limit_bytes=8 * MIB),
        cost_estimate=cost(1_000_000, 500_000),
    )(shares)


def on_device(q_nope, q_rope, latent, k_rope, d_out, advantage, segment, w_uk, w_uv):
    rows, width = q_nope.shape
    piece = w_uk.shape[0]
    count = lax.axis_size("ctx")
    ring = 4
    steps = count // (2 * ring)
    place = lax.axis_index("ctx").reshape(1)

    def device(step, place, core):
        return (step * ring + place) * 2 + core

    along_y = [
        [device(step, place, core) for place in range(ring)]
        for step in range(steps)
        for core in range(2)
    ]
    along_z = [
        [device(step, place, core) for step in range(steps) for core in range(2)]
        for place in range(ring)
    ]

    def swapped(value):
        return lax.ppermute(value, "ctx", [(source, source ^ 1) for source in range(count)])

    def to_chip(value, chips):
        pairs = [(source, source + 2 * chips) for source in range(count)]
        return lax.ppermute(value, "ctx", [pair for pair in pairs if 0 <= pair[1] < count])

    def exchanged(value, groups):
        return lax.all_to_all(value, "ctx", 0, 0, axis_index_groups=groups, tiled=True)

    column = exchanged(slots(w_uk, w_uv, 2 * steps), along_z)
    keys = jnp.concatenate([latent, k_rope], axis=1)
    near = jnp.stack([to_chip(keys, 2), to_chip(keys, 1), keys])
    column, near = lax.optimization_barrier((column, near))
    spread = jnp.broadcast_to(column[None], (ring,) + column.shape)
    weights = exchanged(spread, along_y).reshape(ring, steps, 2, piece, width)
    far = swapped(near)
    kept, lent = split_heads(place, advantage.reshape(1, rows), q_nope, q_rope, d_out)
    borrowed = swapped(lent)

    d_kept, d_lent, grad_kept, grad_given, d_weights = layer(
        place, segment.reshape(count, rows), kept, borrowed, near, far, weights
    )

    got = swapped(grad_given)
    sums = grad_kept.astype(jnp.float32) + got.astype(jnp.float32)
    far_sum = sums[0].astype(jnp.bfloat16)
    shares = exchanged(d_weights, along_y)
    near_sum = sums[1].astype(jnp.bfloat16)
    total = sums[2] + to_chip(near_sum, -1).astype(jnp.float32)
    total = (total + to_chip(far_sum, -2).astype(jnp.float32)).astype(jnp.bfloat16)
    shares, total = lax.optimization_barrier((shares, total))
    heads_over = lax.axis_size("head")
    key_terms = lax.all_to_all(total, "head", 0, 0, tiled=True)
    d_column = jnp.sum(shares.astype(jnp.float32), axis=0).astype(jnp.bfloat16)
    key_terms, d_column = lax.optimization_barrier((key_terms, d_column))
    returned = swapped(d_lent)
    d_q_nope, d_q_rope = join_heads(place, d_kept, returned, width, q_rope.shape[1])
    d_shares = exchanged(d_column.reshape(2 * steps, piece, width), along_z)
    key_terms = key_terms.reshape(heads_over, rows // heads_over, LAT + ROPE)
    d_latent, d_k_rope = summed(key_sum_kernel, key_terms, rows // heads_over, (LAT, ROPE))
    d_uk, d_uv = summed(
        up_sum_kernel, d_shares.reshape(steps, 2, piece, width), piece, (width, width)
    )
    return (d_q_nope, d_q_rope, d_latent, d_k_rope, d_uk, d_uv)


def solution(mesh):
    placed = (
        P("ctx", "head"),
        P("ctx", "head"),
        P("ctx", None),
        P("ctx", None),
        P("ctx", "head"),
        P("ctx"),
        P(),
        P("ctx", "head"),
        P("ctx", "head"),
    )
    return jax.shard_map(
        on_device,
        mesh=mesh,
        in_specs=placed,
        out_specs=(
            P("ctx", "head"),
            P("ctx", "head"),
            P(("ctx", "head"), None),
            P(("ctx", "head"), None),
            P("ctx", "head"),
            P("ctx", "head"),
        ),
        check_vma=False,
    )
```
